32 devices in a mesh: groups: 2 (over x), node: 16 (over z, y, core).
Axes of the slice: x: 2, y: 2, z: 4, core: 2. Of those that a mesh axis runs over, the one named last changes fastest.
Arguments:
- node_latent: bfloat16 [6144, 512], P(('groups', 'node')), parts along dimension 0, may hold values from -6 to 6
- edge_latent: bfloat16 [49152, 512], P(('groups', 'node')), parts along dimension 0, may hold values from -6 to 6
- node_cotangent: bfloat16 [6144, 512], P(('groups', 'node')), parts along dimension 0, may hold values from -6 to 6
- edge_cotangent: bfloat16 [49152, 512], P(('groups', 'node')), parts along dimension 0, may hold values from -6 to 6
- sender_slot: int32 [49152], P(('groups', 'node')), parts along dimension 0, may hold values from 0 to 319, as said below
- receiver: int32 [49152], P(('groups', 'node')), parts along dimension 0, may hold values from 0 to 191
- send_index: int32 [32, 16, 8], P(('groups', 'node')), parts along dimension 0, may hold values from 0 to 192, as said below
- edge_w1: bfloat16 [1536, 512], replicated, may hold values from -0.15625 to 0.15625
- edge_w2: bfloat16 [512, 512], replicated, may hold values from -0.25 to 0.25
- edge_gain: float32 [512], replicated, may hold values from 0.1 to 1.9
- node_w1: bfloat16 [1024, 512], replicated, may hold values from -0.1875 to 0.1875
- node_w2: bfloat16 [512, 512], replicated, may hold values from -0.25 to 0.25
- node_gain: float32 [512], replicated, may hold values from 0.1 to 1.9
Outputs:
- node_grad: bfloat16 [6144, 512], P(('groups', 'node')), parts along dimension 0
- edge_grad: bfloat16 [49152, 512], P(('groups', 'node')), parts along dimension 0
- edge_w1_grad: float32 [3072, 512], P(('groups', 'node')), parts along dimension 0
- edge_w2_grad: float32 [1024, 512], P(('groups', 'node')), parts along dimension 0
- edge_gain_grad: float32 [1024], P(('groups', 'node')), parts along dimension 0
- node_w1_grad: float32 [2048, 512], P(('groups', 'node')), parts along dimension 0
- node_w2_grad: float32 [1024, 512], P(('groups', 'node')), parts along dimension 0
- node_gain_grad: float32 [1024], P(('groups', 'node')), parts along dimension 0
The draws below stay inside these ranges and needn't reach their ends.
There are 2 independent parts, one for each index of `groups`. The reference program is written for one: setup_inputs(seed, part) draws one part's arguments, and reference() takes and returns one part's arrays. A program takes and returns all parts, laid end to end along the dimension named above; an argument that names none is the same for every part. Nothing has to cross between parts.
Inputs may be any that keep to these rules, and one draw needn't show every extreme that they name: send_index[d, p, c] is the index within device d's block of the node that d sends to device p in slot c, and 192 marks an empty slot; the filled slots of a pair come first, a device sends nothing to itself, and the pair from device 16 - 1 to device 0 fills all 8 slots. `sender_slot`: for an edge on device p, a value v below 192 names node v of p's block; a value 192 + d * 8 + c names slot c of what device d sends to p, which is always a filled slot, and every filled slot is named by some edge of p.
All inputs are finite; a program needn't handle non-finite values.
Results may differ from the reference program's by a relative error of at most 0.008.
Values may be sent and summed in bfloat16 or wider, within the bound.
A program may use at most 128 MiB of HBM per device.

```python
import math
import jax
import jax.numpy as jnp
from jax import lax

D = 512
NODE_DEV = 192
CAP = 8
EDGE_DEV = 1536
NODES = 3072
EDGES = 24576
N_NODE = 16


def shared_graph(key):
    keys = jax.random.split(key, 3)
    ids = jnp.arange(N_NODE, dtype=jnp.int32)
    load = jax.random.randint(keys[0], (N_NODE,), 1, 5)
    raw = jax.random.randint(keys[1], (N_NODE, N_NODE), 0, 2 * CAP + 1)
    count = jnp.minimum(CAP, raw * load[None, :] // 4)
    count = jnp.where(ids[:, None] == ids[None, :], 0, count)
    count = jnp.where((ids[:, None] == N_NODE - 1) & (ids[None, :] == 0), CAP, count)
    picks = jax.random.randint(keys[2], (N_NODE, N_NODE, CAP), 0, NODE_DEV)
    live = jnp.arange(CAP, dtype=jnp.int32)[None, None, :] < count[:, :, None]
    sends = jnp.where(live, picks, NODE_DEV)
    return (live, sends)


def draw_send_index(key, part):
    live, sends = shared_graph(key)
    return sends.astype(jnp.int32)


def draw_sender_slot(key, part):
    live, sends = shared_graph(key)
    key = jax.random.fold_in(key, 7)
    slots = N_NODE * CAP

    def per_device(owner, subkey):
        flat = live[:, owner, :].reshape(slots)
        order = jnp.argsort(jnp.where(flat, 0, 1), stable=True).astype(jnp.int32)
        total = jnp.sum(flat.astype(jnp.int32))
        keys = jax.random.split(subkey, 4)
        position = jnp.arange(EDGE_DEV, dtype=jnp.int32)
        coin = jax.random.randint(keys[0], (EDGE_DEV,), 0, 2)
        local_pick = jax.random.randint(keys[1], (EDGE_DEV,), 0, NODE_DEV)
        halo_pick = order[jax.random.randint(keys[2], (EDGE_DEV,), 0, slots) % jnp.maximum(total, 1)]
        other = jnp.where((coin == 0) | (total == 0), local_pick, NODE_DEV + halo_pick)
        chosen = jnp.where(position < total, NODE_DEV + order[jnp.minimum(position, slots - 1)], other)
        shuffle = jax.random.permutation(keys[3], EDGE_DEV)
        return chosen[shuffle]
    owners = jnp.arange(N_NODE, dtype=jnp.int32)
    result = jax.vmap(per_device)(owners, jax.random.split(key, N_NODE))
    return result.reshape(N_NODE * EDGE_DEV).astype(jnp.int32)


def plant(entries, stream_key, least, top_value):
    longest = entries.shape.index(max(entries.shape))
    spots = []
    for shift in (0, 1):
        where = [jax.random.randint(jax.random.fold_in(stream_key, axis), (), 0, length) for axis, length in enumerate(entries.shape)]
        where[longest] = (where[longest] + shift) % entries.shape[longest]
        spots.append(tuple(where))
    return entries.at[spots[0]].set(least).at[spots[1]].set(top_value)


def strengthened(array, rng, source, target, parts, factor):
    owner, partner = [(jnp.arange(array.shape[dim]) // (array.shape[dim] // parts)).reshape([-1 if axis == dim else 1 for axis in range(array.ndim)]) for dim in (source, target)]
    chosen = jax.random.permutation(rng, parts)[partner]
    strong = (owner == chosen) | (owner == (partner + parts // 2) % parts)
    return jnp.where(strong, factor * array, array)


def block_levels(rng, extent, cuts, least, top_value):
    factor_of = 1.0
    for dim, blocks in cuts:
        heights = jax.random.uniform(jax.random.fold_in(jax.random.fold_in(rng, 6), dim), (blocks,), jnp.float32, least / len(cuts), top_value / len(cuts))
        factor_of = factor_of * jnp.repeat(jnp.exp(heights), extent[dim] // blocks).reshape((-1,) + (1,) * (len(extent) - 1 - dim))
    return factor_of


def bell_draw(rng, shape, deviation, bound, shards=(), held_as=jnp.bfloat16):
    values = deviation * jax.random.normal(rng, shape, jnp.float32)
    if shards:
        values = values * block_levels(rng, shape, shards, -0.22, 0.18)
    return jnp.clip(values, -bound, bound).astype(held_as)


def noise_with(own_key, extent, deviation, limit, cuts, heavy, kind=jnp.bfloat16):
    values = deviation * jax.random.normal(own_key, extent, jnp.float32)
    if cuts:
        values = values * block_levels(own_key, extent, cuts, -0.22, 0.18)
    return jnp.clip(strengthened(values, jax.random.fold_in(own_key, 3), *heavy), -limit, limit).astype(kind)


def setup_inputs(seed: int = 0, part: int = 0) -> dict:
    arg_keys = jax.random.split(jax.random.key(seed), 14)
    part_splits = jax.random.split(jax.random.fold_in(arg_keys[13], part), 14)
    node_latent = bell_draw(part_splits[0], (NODES, D), 1.0, 6.0, ((0, 16),))
    edge_latent = noise_with(part_splits[1], (EDGES, D), 1.0, 6.0, ((0, 16),), (0, 1, 16, 2.0))
    node_cotangent = bell_draw(part_splits[2], (NODES, D), 1.0, 6.0, ((0, 16),))
    edge_cotangent = bell_draw(part_splits[3], (EDGES, D), 1.0, 6.0, ((0, 16),))
    sender_slot = draw_sender_slot(jax.random.fold_in(jax.random.fold_in(arg_keys[13], part), 71), part)
    receiver = plant(jax.random.randint(part_splits[5], (EDGES,), 0, NODE_DEV), jax.random.fold_in(part_splits[5], 1), 0, NODE_DEV - 1).astype(jnp.int32)
    send_index = draw_send_index(jax.random.fold_in(jax.random.fold_in(arg_keys[13], part), 71), part)
    edge_w1 = bell_draw(arg_keys[7], (3 * D, D), (3 * D) ** -0.5, 0.15625)
    edge_w2 = bell_draw(arg_keys[8], (D, D), D ** -0.5, 0.25)
    edge_gain = jnp.clip(1.0 + 0.18 * jax.random.normal(arg_keys[9], (D,), jnp.float32), 0.1, 1.9)
    node_w1 = bell_draw(arg_keys[10], (2 * D, D), (2 * D) ** -0.5, 0.1875)
    node_w2 = bell_draw(arg_keys[11], (D, D), D ** -0.5, 0.25)
    node_gain = jnp.clip(1.0 + 0.18 * jax.random.normal(arg_keys[12], (D,), jnp.float32), 0.1, 1.9)
    return dict(node_latent=node_latent, edge_latent=edge_latent, node_cotangent=node_cotangent, edge_cotangent=edge_cotangent, sender_slot=sender_slot, receiver=receiver, send_index=send_index, edge_w1=edge_w1, edge_w2=edge_w2, edge_gain=edge_gain, node_w1=node_w1, node_w2=node_w2, node_gain=node_gain)


def normalize(values):
    mean = lax.optimization_barrier(jnp.mean(values, axis=-1, keepdims=True))
    centred = values - mean
    inverse = lax.rsqrt(lax.optimization_barrier(jnp.mean(centred * centred, axis=-1, keepdims=True)) + 1e-05)
    return (centred * inverse, inverse)

def norm_back(grad, normed, inverse, gain):
    scaled = grad * gain
    first = lax.optimization_barrier(jnp.mean(scaled, axis=-1, keepdims=True))
    second = lax.optimization_barrier(jnp.mean(scaled * normed, axis=-1, keepdims=True))
    return inverse * (scaled - first - normed * second)

def silu_back(grad, pre):
    sig = jax.nn.sigmoid(pre)
    return grad * sig * (1.0 + pre * (1.0 - sig))

def contract_rows(left, right):
    return lax.dot_general(left, right, (((0,), (0,)), ((), ())), preferred_element_type=jnp.float32)

def contract_cols(left, right):
    return lax.dot_general(left, right, (((1,), (1,)), ((), ())), preferred_element_type=jnp.float32)

def reference(node_latent, edge_latent, node_cotangent, edge_cotangent, sender_slot, receiver, send_index, edge_w1, edge_w2, edge_gain, node_w1, node_w2, node_gain):
    nodes = NODE_DEV * N_NODE
    edges = EDGE_DEV * N_NODE
    owner = (jnp.arange(edges, dtype=jnp.int32) // EDGE_DEV).astype(jnp.int32)
    local = sender_slot < NODE_DEV
    halo = jnp.maximum(sender_slot - NODE_DEV, 0).astype(jnp.int32)
    source = (halo // CAP).astype(jnp.int32)
    place = (halo % CAP).astype(jnp.int32)
    remote = send_index[source, owner, place]
    sender = jnp.where(local, owner * NODE_DEV + sender_slot, source * NODE_DEV + remote).astype(jnp.int32)
    target = (owner * NODE_DEV + receiver).astype(jnp.int32)

    def edge_forward(latent, send_ids, recv_ids):
        joined = jnp.concatenate([latent, node_latent[send_ids], node_latent[recv_ids]], axis=1)
        pre = jnp.dot(joined, edge_w1, preferred_element_type=jnp.float32)
        hidden = (pre * jax.nn.sigmoid(pre)).astype(jnp.bfloat16)
        out = jnp.dot(hidden, edge_w2, preferred_element_type=jnp.float32)
        normed, inverse = normalize(out)
        return (joined, pre, hidden, normed, inverse)
    blocks_e = edge_latent.reshape(N_NODE, EDGE_DEV, D)
    blocks_s = sender.reshape(N_NODE, EDGE_DEV)
    blocks_t = target.reshape(N_NODE, EDGE_DEV)
    blocks_c = edge_cotangent.reshape(N_NODE, EDGE_DEV, D)

    def first_pass(inputs):
        latent, send_ids, recv_ids = inputs
        joined, pre, hidden, normed, inverse = edge_forward(latent, send_ids, recv_ids)
        return (latent.astype(jnp.float32) + normed * edge_gain).astype(jnp.bfloat16)
    updated = lax.map(first_pass, (blocks_e, blocks_s, blocks_t)).reshape(edges, D)
    aggregate = jax.ops.segment_sum(updated.astype(jnp.float32), target, num_segments=nodes).astype(jnp.bfloat16)
    node_input = jnp.concatenate([node_latent, aggregate], axis=1)
    node_pre = jnp.dot(node_input, node_w1, preferred_element_type=jnp.float32)
    node_hidden = (node_pre * jax.nn.sigmoid(node_pre)).astype(jnp.bfloat16)
    node_out = jnp.dot(node_hidden, node_w2, preferred_element_type=jnp.float32)
    node_hat, node_inv = normalize(node_out)
    node_dy = node_cotangent.astype(jnp.float32)
    node_scale = 1.0 / math.sqrt(nodes)
    node_gain_grad = lax.optimization_barrier(jnp.sum(node_dy * node_hat, axis=0)) * node_scale
    node_mgrad = norm_back(node_dy, node_hat, node_inv, node_gain).astype(jnp.bfloat16)
    node_w2_grad = contract_rows(node_hidden, node_mgrad) * node_scale
    node_agrad = silu_back(contract_cols(node_mgrad, node_w2), node_pre).astype(jnp.bfloat16)
    node_w1_grad = contract_rows(node_input, node_agrad) * node_scale
    node_xgrad = contract_cols(node_agrad, node_w1)
    agg_grad = node_xgrad[:, D:]

    def second_pass(carry, inputs):
        w1_sum, w2_sum, gain_sum, node_sum = carry
        latent, send_ids, recv_ids, cotangent = inputs
        joined, pre, hidden, normed, inverse = edge_forward(latent, send_ids, recv_ids)
        total = cotangent.astype(jnp.float32) + agg_grad[recv_ids]
        gain_sum = gain_sum + lax.optimization_barrier(jnp.sum(total * normed, axis=0))
        mgrad = norm_back(total, normed, inverse, edge_gain).astype(jnp.bfloat16)
        w2_sum = w2_sum + contract_rows(hidden, mgrad)
        agrad = silu_back(contract_cols(mgrad, edge_w2), pre).astype(jnp.bfloat16)
        w1_sum = w1_sum + contract_rows(joined, agrad)
        xgrad = contract_cols(agrad, edge_w1)
        node_sum = node_sum.at[send_ids].add(xgrad[:, D:2 * D]).at[recv_ids].add(xgrad[:, 2 * D:])
        grad_out = (total + xgrad[:, :D]).astype(jnp.bfloat16)
        return ((w1_sum, w2_sum, gain_sum, node_sum), grad_out)
    start = (jnp.zeros((3 * D, D), jnp.float32), jnp.zeros((D, D), jnp.float32), jnp.zeros((D,), jnp.float32), jnp.zeros((nodes, D), jnp.float32))
    (w1_sum, w2_sum, gain_sum, node_sum), edge_blocks = lax.scan(second_pass, start, (blocks_e, blocks_s, blocks_t, blocks_c))
    edge_scale = 1.0 / math.sqrt(edges)
    node_grad = (node_dy + node_xgrad[:, :D] + node_sum).astype(jnp.bfloat16)
    edge_grad = edge_blocks.reshape(edges, D)
    return (node_grad, edge_grad, w1_sum * edge_scale, w2_sum * edge_scale, gain_sum * edge_scale, node_w1_grad, node_w2_grad, node_gain_grad)
```

```python
import functools
import math

import jax
import jax.numpy as jnp
from jax import lax
from jax.experimental import pallas as pl
from jax.experimental.pallas import tpu as pltpu
from jax.sharding import PartitionSpec as P

F32 = jnp.float32
BF16 = jnp.bfloat16
MESH = pl.DeviceIdType.MESH
VMEM_LIMIT = 56 * 1024 * 1024
CHUNK = 256


def mm(left, right):
    return jnp.dot(left, right, preferred_element_type=F32)


def mm_rows(left, right):
    return lax.dot_general(left, right, (((0,), (0,)), ((), ())), preferred_element_type=F32)


def mm_cols(left, right):
    return lax.dot_general(left, right, (((1,), (1,)), ((), ())), preferred_element_type=F32)


def pack(rows):
    cap, half = rows.shape[1], rows.shape[2] // 2
    return jnp.concatenate([rows[:, :, :half], rows[:, :, half:]], axis=1).astype(BF16)


def unpack(packed):
    n, cap = packed.shape[0], packed.shape[1] // 2
    wide = packed.astype(F32)
    both = jnp.concatenate([wide[:, :cap, :], wide[:, cap:, :]], axis=2)
    return both.reshape(n * cap, both.shape[2])


def swap_blocks(n, me, src, dst, send_sem, recv_sem):
    def copy_to(peer):
        return pltpu.make_async_remote_copy(
            src_ref=src.at[peer],
            dst_ref=dst.at[me],
            send_sem=send_sem.at[peer],
            recv_sem=recv_sem.at[me],
            device_id={"node": peer},
            device_id_type=MESH,
        )

    def copy_from(peer):
        return pltpu.make_async_remote_copy(
            src_ref=src.at[peer],
            dst_ref=dst.at[peer],
            send_sem=send_sem.at[peer],
            recv_sem=recv_sem.at[peer],
            device_id={"node": peer},
            device_id_type=MESH,
        )

    def start():
        @pl.loop(1, n)
        def _(k):
            copy_to(lax.rem(me + k, n)).start()

    def wait_recv():
        @pl.loop(1, n)
        def _(k):
            copy_from(lax.rem(me + k, n)).wait_recv()

    def wait_send():
        @pl.loop(1, n)
        def _(k):
            copy_from(lax.rem(me + k, n)).wait_send()

    return start, wait_recv, wait_send


def greet_all(n, me):
    barrier = pltpu.get_barrier_semaphore()

    @pl.loop(1, n)
    def _(k):
        pl.semaphore_signal(
            barrier, inc=1, device_id={"node": lax.rem(me + k, n)}, device_id_type=MESH
        )

    pl.semaphore_wait(barrier, n - 1)


def halo_kernel(n, index_ref, node_ref, in_ref, out_buf, in_buf, send_sem, recv_sem):
    me = lax.axis_index("node")
    nodes = node_ref.shape[0]
    slots = index_ref.shape[0]
    pick = (
        index_ref[...] == lax.broadcasted_iota(jnp.int32, (slots, nodes), 1)
    ).astype(F32).astype(BF16)
    rows = mm(pick, node_ref[...])
    out_buf[...] = pack(rows.reshape(n, slots // n, rows.shape[1]))
    in_buf[me] = jnp.zeros(in_buf.shape[1:], BF16)
    greet_all(n, me)
    start, wait_recv, wait_send = swap_blocks(n, me, out_buf, in_buf, send_sem, recv_sem)
    start()
    wait_recv()
    in_ref[...] = in_buf[...]
    wait_send()


def norm_back(grad, normed, inverse, gain):
    scaled = grad * gain
    first = jnp.mean(scaled, axis=-1, keepdims=True)
    second = jnp.mean(scaled * normed, axis=-1, keepdims=True)
    return inverse * (scaled - first - normed * second)


def normalize(values):
    mean = jnp.mean(values, axis=-1, keepdims=True)
    centred = values - mean
    inverse = lax.rsqrt(jnp.mean(centred * centred, axis=-1, keepdims=True) + 1e-05)
    return centred * inverse, inverse


def silu_parts(pre):
    sig = jax.nn.sigmoid(pre)
    return (pre * sig).astype(BF16), sig * (1.0 + pre * (1.0 - sig))


def bit_orders(n):
    bits = n.bit_length() - 1
    cut = 1 + (bits - 1) // 2
    low, high = list(range(1, cut)), list(range(cut, bits))
    return [0] + low + high, [0] + high + low


def place_of(d, order):
    place = 0
    for bit in order:
        place = 2 * place + ((d >> bit) & 1)
    return place


def layer_kernel(
    n,
    rows_of,
    node_scale,
    edge_scale,
    node_ref,
    halo_ref,
    latent_ref,
    node_cot_ref,
    cot_ref,
    send_col,
    recv_col,
    send_row,
    recv_row,
    w1_ref,
    w2_ref,
    gain_ref,
    nw1_ref,
    nw2_ref,
    ngain_ref,
    edge_out,
    first_out,
    second_out,
    slot_out,
    base_out,
    table,
    proj,
    pick,
    pick_t,
    slope,
    hidden,
    hat,
    inv,
    rows_bf,
    agrad,
    agg_bf,
    gain_sum,
    grad_w1,
    grad_w2,
    grad_n1,
    grad_n2,
):
    nodes, width = node_ref.shape
    edges = latent_ref.shape[0]
    slots = table.shape[0]
    total_cols = slots + nodes
    steps = edges // CHUNK
    node = node_ref[...]
    table[:nodes, :] = node
    table[nodes:, :] = unpack(halo_ref[...]).astype(BF16)
    proj[:slots, :] = mm(table[...], w1_ref[width : 2 * width, :]).astype(BF16)
    proj[slots:, :] = mm(node, w1_ref[2 * width :, :]).astype(BF16)

    row_id = lax.broadcasted_iota(jnp.int32, (slots, edges), 0)
    pick_t[:slots, :] = (row_id == send_row[...]).astype(F32).astype(BF16)
    row_id = lax.broadcasted_iota(jnp.int32, (nodes, edges), 0)
    pick_t[slots:, :] = (row_id == recv_row[...]).astype(F32).astype(BF16)

    @pl.loop(0, steps)
    def _(step):
        here = pl.ds(pl.multiple_of(step * CHUNK, CHUNK), CHUNK)
        col_id = lax.broadcasted_iota(jnp.int32, (CHUNK, total_cols), 1)
        chosen = (col_id == send_col[here, :]) | (col_id == recv_col[here, :] + slots)
        one_hot = chosen.astype(F32).astype(BF16)
        pick[here, :] = one_hot
        latent = latent_ref[here, :]
        pre = mm(latent, w1_ref[:width, :]) + mm(one_hot, proj[...])
        hid, slope_here = silu_parts(pre)
        hidden[here, :] = hid
        slope[here, :] = slope_here
        hat_here, inv_here = normalize(mm(hid, w2_ref[...]))
        hat[here, :] = hat_here
        inv[here, :] = inv_here
        rows_bf[here, :] = (latent.astype(F32) + hat_here * gain_ref[...]).astype(BF16)

    aggregate = mm(pick_t[slots:, :], rows_bf[...]).astype(BF16)
    node_pre = mm(node, nw1_ref[:width, :]) + mm(aggregate, nw1_ref[width:, :])
    node_hidden, node_slope = silu_parts(node_pre)
    node_hat, node_inv = normalize(mm(node_hidden, nw2_ref[...]))
    node_dy = node_cot_ref[...].astype(F32)
    node_gain_part = jnp.sum(node_dy * node_hat, axis=0, keepdims=True) * node_scale
    node_mgrad = norm_back(node_dy, node_hat, node_inv, ngain_ref[...]).astype(BF16)
    grad_n2[...] = mm_rows(node_hidden, node_mgrad)
    node_agrad = (mm_cols(node_mgrad, nw2_ref[...]) * node_slope).astype(BF16)
    grad_n1[:width, :] = mm_rows(node, node_agrad)
    grad_n1[width:, :] = mm_rows(aggregate, node_agrad)
    agg_bf[...] = mm_cols(node_agrad, nw1_ref[width:, :]).astype(BF16)
    base_out[...] = node_dy + mm_cols(node_agrad, nw1_ref[:width, :])
    gain_sum[...] = jnp.zeros_like(gain_sum)

    @pl.loop(0, steps)
    def _(step):
        here = pl.ds(pl.multiple_of(step * CHUNK, CHUNK), CHUNK)
        col_id = lax.broadcasted_iota(jnp.int32, (CHUNK, nodes), 1)
        incidence = (col_id == recv_col[here, :]).astype(F32).astype(BF16)
        total = cot_ref[here, :].astype(F32) + mm(incidence, agg_bf[...])
        hat_here = hat[here, :]
        product = total * hat_here
        gain_sum[...] += jnp.sum(product.reshape(CHUNK // 8, 8, width), axis=0)
        mgrad = norm_back(total, hat_here, inv[here, :], gain_ref[...]).astype(BF16)
        rows_bf[here, :] = mgrad
        ag = (mm_cols(mgrad, w2_ref[...]) * slope[here, :]).astype(BF16)
        agrad[here, :] = ag
        edge_out[here, :] = (total + mm_cols(ag, w1_ref[:width, :])).astype(BF16)

    edge_gain_part = jnp.sum(gain_sum[...], axis=0, keepdims=True) * edge_scale
    grad_w2[...] = mm_rows(hidden[...], rows_bf[...])
    grad_w1[:width, :] = mm_rows(latent_ref[...], agrad[...])
    sums = mm(pick_t[...], agrad[...]).astype(BF16)
    by_slot, by_target = sums[:slots, :], sums[slots:, :]
    grad_w1[width : 2 * width, :] = mm_rows(table[...], by_slot)
    grad_w1[2 * width :, :] = mm_rows(node, by_target)
    slot_sums = mm_cols(by_slot, w1_ref[width : 2 * width, :])
    base_out[...] += slot_sums[:nodes, :] + mm_cols(by_target, w1_ref[2 * width :, :])
    remote = slot_sums[nodes:, :]
    slot_out[...] = pack(remote.reshape(n, remote.shape[0] // n, width))

    half = width // 2
    used = sum(rows_of)
    spare = first_out.shape[1] - used
    row_id = lax.broadcasted_iota(jnp.int32, (spare, width), 0)
    tail = jnp.where(row_id == 0, edge_gain_part, jnp.where(row_id == 1, node_gain_part, 0.0))
    sources = (
        (grad_w1, edge_scale),
        (grad_w2, edge_scale),
        (grad_n1, node_scale),
        (grad_n2, node_scale),
    )
    for order, out, cols in zip(
        bit_orders(n), (first_out, second_out), (slice(0, half), slice(half, width))
    ):
        for d in range(n):
            pieces = []
            for (source, scale), rows in zip(sources, rows_of):
                pieces.append(source[d * rows : (d + 1) * rows, cols] * scale)
            pieces.append(tail[:, cols])
            out[place_of(d, order)] = jnp.concatenate(pieces, axis=0).astype(BF16)


def sum_kernel(
    n,
    rows_of,
    first_ref,
    second_ref,
    slot_ref,
    base_ref,
    index_ref,
    node_out,
    w1_out,
    w2_out,
    n1_out,
    n2_out,
    gain_out,
    *scratch,
):
    me = lax.axis_index("node")
    bits = n.bit_length() - 1
    held = [first_ref, second_ref]
    landing = (scratch[:bits], scratch[bits : 2 * bits])
    slot_in, send_sem, recv_sem, halo_send, halo_recv = scratch[2 * bits :]
    greet_all(n, me)
    start, wait_recv, wait_send = swap_blocks(n, me, slot_ref, slot_in, halo_send, halo_recv)
    orders = bit_orders(n)
    copies = {}
    bases = [0, 0]

    def launch(path, level):
        bit = orders[path][level]
        mine = lax.rem(me // (1 << bit), 2)
        size = n >> (level + 1)
        peer = me + (1 - 2 * mine) * (1 << bit)
        source = held[path].at[pl.ds(bases[path] + (1 - mine) * size, size)]
        bases[path] = bases[path] + mine * size
        copy = pltpu.make_async_remote_copy(
            src_ref=source,
            dst_ref=landing[path][level],
            send_sem=send_sem.at[path, level],
            recv_sem=recv_sem.at[path, level],
            device_id={"node": peer},
            device_id_type=MESH,
        )
        copy.start()
        copies[path, level] = copy

    launch(0, 0)
    launch(1, 0)
    start()
    half = first_ref.shape[2]
    for level in range(bits):
        for path in range(2):
            copies[path, level].wait_recv()
            size = n >> (level + 1)
            base = bases[path]
            if level < bits - 1:

                @pl.loop(0, size)
                def _(k):
                    landing[path][level][k] = (
                        held[path][base + k].astype(F32) + landing[path][level][k].astype(F32)
                    ).astype(BF16)

                held[path] = landing[path][level]
                bases[path] = 0
                launch(path, level + 1)
            else:
                cols = slice(path * half, (path + 1) * half)
                done = held[path][base].astype(F32) + landing[path][level][0].astype(F32)
                at = 0
                for out, rows in zip((w1_out, w2_out, n1_out, n2_out), rows_of):
                    out[:, cols] = done[at : at + rows, :]
                    at += rows
                gain_out[:, cols] = done[at : at + 2, :]
    slot_in[me] = jnp.zeros(slot_in.shape[1:], BF16)
    wait_recv()
    nodes = base_ref.shape[0]
    slots = index_ref.shape[1]
    owner = (
        lax.broadcasted_iota(jnp.int32, (nodes, slots), 0) == index_ref[...]
    ).astype(F32).astype(BF16)
    back = mm(owner, unpack(slot_in[...]).astype(BF16))
    node_out[...] = (base_ref[...] + back).astype(BF16)
    for copy in copies.values():
        copy.wait_send()
    wait_send()


def local(
    n,
    node_latent,
    edge_latent,
    node_cotangent,
    edge_cotangent,
    sender_slot,
    receiver,
    send_index,
    edge_w1,
    edge_w2,
    edge_gain,
    node_w1,
    node_w2,
    node_gain,
):
    nodes, width = node_latent.shape
    edges = edge_latent.shape[0]
    cap = send_index.shape[2]
    half = width // 2
    bits = n.bit_length() - 1
    node_scale = 1.0 / math.sqrt(nodes * n)
    edge_scale = 1.0 / math.sqrt(edges * n)
    rows_of = tuple(w.shape[0] // n for w in (edge_w1, edge_w2, node_w1, node_w2))
    block = -(-(sum(rows_of) + 2) // 16) * 16
    slots = nodes + n * cap
    vmem = pl.BlockSpec(memory_space=pltpu.VMEM)
    packed = jax.ShapeDtypeStruct((n, 2 * cap, half), BF16)
    stack = jax.ShapeDtypeStruct((n, block, half), BF16)

    incoming = pl.pallas_call(
        functools.partial(halo_kernel, n),
        out_shape=packed,
        in_specs=[vmem] * 2,
        out_specs=vmem,
        scratch_shapes=[
            pltpu.VMEM(packed.shape, BF16),
            pltpu.VMEM(packed.shape, BF16),
            pltpu.SemaphoreType.DMA((n,)),
            pltpu.SemaphoreType.DMA((n,)),
        ],
        compiler_params=pltpu.CompilerParams(
            collective_id=0, has_side_effects=True, vmem_limit_bytes=VMEM_LIMIT
        ),
    )(send_index.reshape(n * cap, 1), node_latent)

    edge_grad, first, second, slot_sums, base = pl.pallas_call(
        functools.partial(layer_kernel, n, rows_of, node_scale, edge_scale),
        out_shape=(
            jax.ShapeDtypeStruct((edges, width), BF16),
            stack,
            stack,
            packed,
            jax.ShapeDtypeStruct((nodes, width), F32),
        ),
        in_specs=[vmem] * 15,
        out_specs=(vmem,) * 5,
        scratch_shapes=[
            pltpu.VMEM((slots, width), BF16),
            pltpu.VMEM((slots + nodes, width), BF16),
            pltpu.VMEM((edges, slots + nodes), BF16),
            pltpu.VMEM((slots + nodes, edges), BF16),
            pltpu.VMEM((edges, width), F32),
            pltpu.VMEM((edges, width), BF16),
            pltpu.VMEM((edges, width), F32),
            pltpu.VMEM((edges, 1), F32),
            pltpu.VMEM((edges, width), BF16),
            pltpu.VMEM((edges, width), BF16),
            pltpu.VMEM((nodes, width), BF16),
            pltpu.VMEM((8, width), F32),
            pltpu.VMEM((3 * width, width), F32),
            pltpu.VMEM((width, width), F32),
            pltpu.VMEM((2 * width, width), F32),
            pltpu.VMEM((width, width), F32),
        ],
        compiler_params=pltpu.CompilerParams(vmem_limit_bytes=VMEM_LIMIT),
    )(
        node_latent,
        incoming,
        edge_latent,
        node_cotangent,
        edge_cotangent,
        sender_slot.reshape(edges, 1),
        receiver.reshape(edges, 1),
        sender_slot.reshape(1, edges),
        receiver.reshape(1, edges),
        edge_w1,
        edge_w2,
        edge_gain.reshape(1, width),
        node_w1,
        node_w2,
        node_gain.reshape(1, width),
    )

    landing = [pltpu.VMEM((n >> (level + 1), block, half), BF16) for level in range(bits)]
    node_grad, w1_grad, w2_grad, n1_grad, n2_grad, gains = pl.pallas_call(
        functools.partial(sum_kernel, n, rows_of),
        out_shape=(jax.ShapeDtypeStruct((nodes, width), BF16),)
        + tuple(jax.ShapeDtypeStruct((rows, width), F32) for rows in rows_of)
        + (jax.ShapeDtypeStruct((2, width), F32),),
        in_specs=[vmem] * 5,
        out_specs=(vmem,) * 6,
        scratch_shapes=landing
        + landing
        + [
            pltpu.VMEM(packed.shape, BF16),
            pltpu.SemaphoreType.DMA((2, bits)),
            pltpu.SemaphoreType.DMA((2, bits)),
            pltpu.SemaphoreType.DMA((n,)),
            pltpu.SemaphoreType.DMA((n,)),
        ],
        compiler_params=pltpu.CompilerParams(
            collective_id=1, has_side_effects=True, vmem_limit_bytes=VMEM_LIMIT
        ),
    )(first, second, slot_sums, base, send_index.reshape(1, n * cap))
    share = width // n
    own = lax.dynamic_slice(gains, (0, lax.axis_index("node") * share), (2, share))
    return node_grad, edge_grad, w1_grad, w2_grad, own[0], n1_grad, n2_grad, own[1]


def solution(mesh):
    rows = P(("groups", "node"), None)
    flat = P(("groups", "node"))
    return jax.shard_map(
        functools.partial(local, mesh.shape["node"]),
        mesh=mesh,
        in_specs=(rows, rows, rows, rows, flat, flat, P(("groups", "node"), None, None))
        + (P(),) * 6,
        out_specs=(rows, rows, rows, rows, flat, rows, rows, flat),
        check_vma=False,
    )
```

```python
import functools
import math

import jax
import jax.numpy as jnp
from jax import lax
from jax.experimental import pallas as pl
from jax.experimental.pallas import tpu as pltpu
from jax.sharding import PartitionSpec as P

F32 = jnp.float32
BF16 = jnp.bfloat16
MESH = pl.DeviceIdType.MESH
VMEM_LIMIT = 56 * 1024 * 1024
CHUNK = 256


def mm(left, right):
    return jnp.dot(left, right, preferred_element_type=F32)


def mm_rows(left, right):
    return lax.dot_general(left, right, (((0,), (0,)), ((), ())), preferred_element_type=F32)


def mm_cols(left, right):
    return lax.dot_general(left, right, (((1,), (1,)), ((), ())), preferred_element_type=F32)


def pack(rows):
    cap, half = rows.shape[1], rows.shape[2] // 2
    return jnp.concatenate([rows[:, :, :half], rows[:, :, half:]], axis=1).astype(BF16)


def unpack(packed):
    n, cap = packed.shape[0], packed.shape[1] // 2
    wide = packed.astype(F32)
    both = jnp.concatenate([wide[:, :cap, :], wide[:, cap:, :]], axis=2)
    return both.reshape(n * cap, both.shape[2])


def swap_blocks(n, me, src, dst, send_sem, recv_sem):
    def copy_to(peer):
        return pltpu.make_async_remote_copy(
            src_ref=src.at[peer],
            dst_ref=dst.at[me],
            send_sem=send_sem.at[peer],
            recv_sem=recv_sem.at[me],
            device_id={"node": peer},
            device_id_type=MESH,
        )

    def copy_from(peer):
        return pltpu.make_async_remote_copy(
            src_ref=src.at[peer],
            dst_ref=dst.at[peer],
            send_sem=send_sem.at[peer],
            recv_sem=recv_sem.at[peer],
            device_id={"node": peer},
            device_id_type=MESH,
        )

    def start():
        @pl.loop(1, n)
        def _(k):
            copy_to(lax.rem(me + k, n)).start()

    def wait_recv():
        @pl.loop(1, n)
        def _(k):
            copy_from(lax.rem(me + k, n)).wait_recv()

    def wait_send():
        @pl.loop(1, n)
        def _(k):
            copy_from(lax.rem(me + k, n)).wait_send()

    return start, wait_recv, wait_send


def greet_all(n, me):
    barrier = pltpu.get_barrier_semaphore()

    @pl.loop(1, n)
    def _(k):
        pl.semaphore_signal(
            barrier, inc=1, device_id={"node": lax.rem(me + k, n)}, device_id_type=MESH
        )

    return barrier


def norm_back(grad, normed, inverse, gain):
    scaled = grad * gain
    first = jnp.mean(scaled, axis=-1, keepdims=True)
    second = jnp.mean(scaled * normed, axis=-1, keepdims=True)
    return inverse * (scaled - first - normed * second)


def normalize(values):
    mean = jnp.mean(values, axis=-1, keepdims=True)
    centred = values - mean
    inverse = lax.rsqrt(jnp.mean(centred * centred, axis=-1, keepdims=True) + 1e-05)
    return centred * inverse, inverse


def silu_parts(pre):
    sig = jax.nn.sigmoid(pre)
    return (pre * sig).astype(BF16), sig * (1.0 + pre * (1.0 - sig))


def bit_orders(n):
    bits = n.bit_length() - 1
    cut = 1 + (bits - 1) // 2
    low, high = list(range(1, cut)), list(range(cut, bits))
    return [0] + low + high, [0] + high + low


def place_of(d, order):
    place = 0
    for bit in order:
        place = 2 * place + ((d >> bit) & 1)
    return place


def layer_kernel(
    n,
    waves,
    node_scale,
    edge_scale,
    index_ref,
    node_ref,
    latent_ref,
    node_cot_ref,
    cot_ref,
    w1_ref,
    w2_ref,
    gain_ref,
    nw1_ref,
    nw2_ref,
    ngain_ref,
    edge_out,
    base_out,
    slot_out,
    node_sum_out,
    w2_sum_out,
    w1_sum_out,
    halo_out,
    halo_in,
    slot_send,
    slot_in,
    table,
    proj,
    pick_t,
    slope,
    hidden,
    hat,
    inv,
    rows_bf,
    agrad,
    agg_bf,
    gain_sum,
    grad_w1,
    grad_w2,
    out_send,
    out_recv,
    back_send,
    back_recv,
    wave_send,
    wave_recv,
    *buffers,
):
    me = lax.axis_index("node")
    barrier = greet_all(n, me)
    grad_n1, grad_n2 = grad_w1, grad_w2
    nodes, width = node_ref.shape
    half = width // 2
    edges = latent_ref.shape[0]
    slots = table.shape[0]
    halo = slots - nodes
    steps = edges // CHUNK
    bits = n.bit_length() - 1
    orders = bit_orders(n)
    stacks = [[buffers[2 * w + p] for p in range(2)] for w in range(3)]
    rest = buffers[6:]
    landing = [
        [[rest[(2 * w + p) * bits + level] for level in range(bits)] for p in range(2)]
        for w in range(3)
    ]
    held = [list(pair) for pair in stacks]
    bases = [[0, 0] for _ in range(3)]
    copies = {}

    def launch(w, path, level):
        bit = orders[path][level]
        mine = lax.rem(me // (1 << bit), 2)
        size = n >> (level + 1)
        peer = me + (1 - 2 * mine) * (1 << bit)
        source = held[w][path].at[pl.ds(bases[w][path] + (1 - mine) * size, size)]
        bases[w][path] = bases[w][path] + mine * size
        copy = pltpu.make_async_remote_copy(
            src_ref=source,
            dst_ref=landing[w][path][level],
            send_sem=wave_send.at[w, path, level],
            recv_sem=wave_recv.at[w, path, level],
            device_id={"node": peer},
            device_id_type=MESH,
        )
        copy.start()
        copies[w, path, level] = copy

    def advance(w, level):
        for path in range(2):
            copies[w, path, level].wait_recv()
            size = n >> (level + 1)
            base = bases[w][path]
            kept, came = held[w][path], landing[w][path][level]
            if level < bits - 1:

                @pl.loop(0, size)
                def _(k):
                    came[k] = (kept[base + k].astype(F32) + came[k].astype(F32)).astype(BF16)

                held[w][path] = came
                bases[w][path] = 0
                launch(w, path, level + 1)
            else:
                cols = slice(path * half, (path + 1) * half)
                out = (node_sum_out, w2_sum_out, w1_sum_out)[w]
                out[:, cols] = kept[base].astype(F32) + came[0].astype(F32)

    def fill(w, sources, tail):
        for path in range(2):
            cols = slice(path * half, (path + 1) * half)
            out = stacks[w][path]
            spare = out.shape[1] - sum(rows for _, _, rows in sources)
            for d in range(n):
                pieces = []
                for source, scale, rows in sources:
                    pieces.append(source[d * rows : (d + 1) * rows, cols] * scale)
                if spare:
                    pieces.append(tail[:spare, cols])
                out[place_of(d, orders[path])] = jnp.concatenate(pieces, axis=0).astype(BF16)
            launch(w, path, 0)

    node = node_ref[...]
    owner = (
        lax.broadcasted_iota(jnp.int32, (nodes, halo), 0) == index_ref[:, 2 * edges :]
    ).astype(F32).astype(BF16)
    halo_out[...] = pack(mm_rows(owner, node).reshape(n, halo // n, width))
    halo_in[me] = jnp.zeros(halo_in.shape[1:], BF16)
    slot_in[me] = jnp.zeros(slot_in.shape[1:], BF16)
    pl.semaphore_wait(barrier, n - 1)
    start, wait_in, wait_out = swap_blocks(n, me, halo_out, halo_in, out_send, out_recv)
    start()

    row_id = lax.broadcasted_iota(jnp.int32, (slots, edges), 0)
    pick_t[:slots, :] = (row_id == index_ref[:, :edges]).astype(F32).astype(BF16)
    row_id = lax.broadcasted_iota(jnp.int32, (nodes, edges), 0)
    pick_t[slots:, :] = (row_id == index_ref[:, edges : 2 * edges]).astype(F32).astype(BF16)

    @pl.loop(0, steps)
    def _(step):
        here = pl.ds(pl.multiple_of(step * CHUNK, CHUNK), CHUNK)
        slope[here, :] = mm(latent_ref[here, :], w1_ref[:width, :])

    def project(rows, value):
        high = value.astype(BF16)
        proj[rows, :width] = high
        proj[rows, width:] = (value - high.astype(F32)).astype(BF16)

    table[:nodes, :] = node
    project(slice(slots, slots + nodes), mm(node, w1_ref[2 * width :, :]))
    wait_in()
    table[nodes:, :] = unpack(halo_in[...]).astype(BF16)
    project(slice(0, slots), mm(table[...], w1_ref[width : 2 * width, :]))

    @pl.loop(0, steps)
    def _(step):
        here = pl.ds(pl.multiple_of(step * CHUNK, CHUNK), CHUNK)
        picked = mm_rows(pick_t[:, here], proj[...])
        pre = slope[here, :] + (picked[:, :width] + picked[:, width:])
        hid, slope_here = silu_parts(pre)
        hidden[here, :] = hid
        slope[here, :] = slope_here
        hat_here, inv_here = normalize(mm(hid, w2_ref[...]))
        hat[here, :] = hat_here
        inv[here, :] = inv_here
        rows_bf[here, :] = (
            latent_ref[here, :].astype(F32) + hat_here * gain_ref[...]
        ).astype(BF16)

    aggregate = mm(pick_t[slots:, :], rows_bf[...]).astype(BF16)
    node_pre = mm(node, nw1_ref[:width, :]) + mm(aggregate, nw1_ref[width:, :])
    node_hidden, node_slope = silu_parts(node_pre)
    node_hat, node_inv = normalize(mm(node_hidden, nw2_ref[...]))
    node_dy = node_cot_ref[...].astype(F32)
    node_gain_part = jnp.sum(node_dy * node_hat, axis=0, keepdims=True) * node_scale
    node_mgrad = norm_back(node_dy, node_hat, node_inv, ngain_ref[...]).astype(BF16)
    grad_n2[...] = mm_rows(node_hidden, node_mgrad)
    node_agrad = (mm_cols(node_mgrad, nw2_ref[...]) * node_slope).astype(BF16)
    grad_n1[:width, :] = mm_rows(node, node_agrad)
    grad_n1[width : 2 * width, :] = mm_rows(aggregate, node_agrad)
    blank = jnp.zeros((16, width), F32)
    n1_rows, n2_rows = 2 * width // n, width // n
    fill(0, ((grad_n1, node_scale, n1_rows), (grad_n2, node_scale, n2_rows)), blank)
    agg_bf[...] = mm_cols(node_agrad, nw1_ref[width:, :]).astype(BF16)
    base_out[...] = node_dy + mm_cols(node_agrad, nw1_ref[:width, :])
    gain_sum[...] = jnp.zeros_like(gain_sum)

    def backward(first, last):
        @pl.loop(first, last)
        def _(step):
            here = pl.ds(pl.multiple_of(step * CHUNK, CHUNK), CHUNK)
            total = cot_ref[here, :].astype(F32) + mm_rows(pick_t[slots:, here], agg_bf[...])
            hat_here = hat[here, :]
            product = total * hat_here
            gain_sum[...] += jnp.sum(product.reshape(CHUNK // 8, 8, width), axis=0)
            mgrad = norm_back(total, hat_here, inv[here, :], gain_ref[...]).astype(BF16)
            rows_bf[here, :] = mgrad
            ag = (mm_cols(mgrad, w2_ref[...]) * slope[here, :]).astype(BF16)
            agrad[here, :] = ag
            edge_out[here, :] = (total + mm_cols(ag, w1_ref[:width, :])).astype(BF16)

    third = steps // 3
    backward(0, third)
    advance(0, 0)
    backward(third, steps)

    edge_gain_part = jnp.sum(gain_sum[...], axis=0, keepdims=True) * edge_scale
    row_id = lax.broadcasted_iota(jnp.int32, (32, width), 0)
    tail = jnp.where(row_id == 0, edge_gain_part, jnp.where(row_id == 1, node_gain_part, 0.0))
    grad_w2[...] = mm_rows(hidden[...], rows_bf[...])
    fill(1, ((grad_w2, edge_scale, width // n),), tail)
    if bits > 2:
        advance(0, 1)
    sums = mm(pick_t[...], agrad[...]).astype(BF16)
    by_slot, by_target = sums[:slots, :], sums[slots:, :]
    slot_sums = mm_cols(by_slot, w1_ref[width : 2 * width, :])
    slot_send[...] = pack(slot_sums[nodes:, :].reshape(n, halo // n, width))
    back, wait_back, wait_sent = swap_blocks(n, me, slot_send, slot_in, back_send, back_recv)
    grad_w1[:width, :] = mm_rows(latent_ref[...], agrad[...])
    grad_w1[width : 2 * width, :] = mm_rows(table[...], by_slot)
    grad_w1[2 * width :, :] = mm_rows(node, by_target)
    fill(2, ((grad_w1, edge_scale, 3 * width // n),), blank)
    back()
    base_out[...] += slot_sums[:nodes, :] + mm_cols(by_target, w1_ref[2 * width :, :])

    level = [2, 0, 0]
    if bits <= 2:
        level[0] = 1
    while min(level) < bits:
        for w in (1, 0, 2):
            if level[w] < bits:
                advance(w, level[w])
                level[w] += 1
    wait_back()
    slot_out[...] = slot_in[...]
    for copy in copies.values():
        copy.wait_send()
    wait_out()
    wait_sent()


def finish_kernel(
    rows_of,
    edge_ref,
    base_ref,
    slot_ref,
    index_ref,
    node_sum,
    w2_sum,
    w1_sum,
    edge_out,
    node_out,
    w1_out,
    w2_out,
    n1_out,
    n2_out,
    sem,
):
    copy = pltpu.make_async_copy(edge_ref, edge_out, sem)
    copy.start()
    r1, r2, r3, r4 = rows_of
    nodes, halo = base_ref.shape[0], slot_ref.shape[0] * slot_ref.shape[1] // 2
    skip = index_ref.shape[1] - halo
    owner = (
        lax.broadcasted_iota(jnp.int32, (nodes, halo), 0) == index_ref[:, skip:]
    ).astype(F32).astype(BF16)
    node_out[...] = (base_ref[...] + mm(owner, unpack(slot_ref[...]).astype(BF16))).astype(BF16)
    w1_out[...] = w1_sum[:r1, :]
    w2_out[...] = w2_sum[:r2, :]
    n1_out[...] = node_sum[:r3, :]
    n2_out[...] = node_sum[r3 : r3 + r4, :]
    copy.wait()


def round_up(rows):
    return -(-rows // 16) * 16


def local(
    n,
    node_latent,
    edge_latent,
    node_cotangent,
    edge_cotangent,
    sender_slot,
    receiver,
    send_index,
    edge_w1,
    edge_w2,
    edge_gain,
    node_w1,
    node_w2,
    node_gain,
):
    nodes, width = node_latent.shape
    edges = edge_latent.shape[0]
    cap = send_index.shape[2]
    half = width // 2
    bits = n.bit_length() - 1
    node_scale = 1.0 / math.sqrt(nodes * n)
    edge_scale = 1.0 / math.sqrt(edges * n)
    rows_of = tuple(w.shape[0] // n for w in (edge_w1, edge_w2, node_w1, node_w2))
    waves = (
        round_up(rows_of[2] + rows_of[3]),
        round_up(rows_of[1] + 2),
        round_up(rows_of[0]),
    )
    slots = nodes + n * cap
    vmem = pl.BlockSpec(memory_space=pltpu.VMEM)
    anywhere = pl.BlockSpec(memory_space=pl.ANY)
    packed = jax.ShapeDtypeStruct((n, 2 * cap, half), BF16)
    indices = jnp.concatenate([sender_slot, receiver, send_index.reshape(n * cap)]).reshape(1, -1)
    stacks = [pltpu.VMEM((n, block, half), BF16) for block in waves for _ in range(2)]
    landing = [
        pltpu.VMEM((n >> (level + 1), block, half), BF16)
        for block in waves
        for _ in range(2)
        for level in range(bits)
    ]

    edge_grad, base, slot_back, node_sum, w2_sum, w1_sum = pl.pallas_call(
        functools.partial(layer_kernel, n, waves, node_scale, edge_scale),
        out_shape=(
            jax.ShapeDtypeStruct((edges, width), BF16),
            jax.ShapeDtypeStruct((nodes, width), F32),
            packed,
        )
        + tuple(jax.ShapeDtypeStruct((block, width), F32) for block in waves),
        in_specs=[vmem] * 11,
        out_specs=(vmem,) * 6,
        scratch_shapes=[pltpu.VMEM(packed.shape, BF16)] * 4
        + [
            pltpu.VMEM((slots, width), BF16),
            pltpu.VMEM((slots + nodes, 2 * width), BF16),
            pltpu.VMEM((slots + nodes, edges), BF16),
            pltpu.VMEM((edges, width), F32),
            pltpu.VMEM((edges, width), BF16),
            pltpu.VMEM((edges, width), F32),
            pltpu.VMEM((edges, 1), F32),
            pltpu.VMEM((edges, width), BF16),
            pltpu.VMEM((edges, width), BF16),
            pltpu.VMEM((nodes, width), BF16),
            pltpu.VMEM((8, width), F32),
            pltpu.VMEM((3 * width, width), F32),
            pltpu.VMEM((width, width), F32),
        ]
        + [pltpu.SemaphoreType.DMA((n,))] * 4
        + [pltpu.SemaphoreType.DMA((3, 2, bits))] * 2
        + stacks
        + landing,
        compiler_params=pltpu.CompilerParams(
            collective_id=0, has_side_effects=True, vmem_limit_bytes=VMEM_LIMIT
        ),
    )(
        indices,
        node_latent,
        edge_latent,
        node_cotangent,
        edge_cotangent,
        edge_w1,
        edge_w2,
        edge_gain.reshape(1, width),
        node_w1,
        node_w2,
        node_gain.reshape(1, width),
    )

    edge_grad, node_grad, w1_grad, w2_grad, n1_grad, n2_grad = pl.pallas_call(
        functools.partial(finish_kernel, rows_of),
        out_shape=(
            jax.ShapeDtypeStruct((edges, width), BF16),
            jax.ShapeDtypeStruct((nodes, width), BF16),
        )
        + tuple(jax.ShapeDtypeStruct((rows, width), F32) for rows in rows_of),
        in_specs=[anywhere] + [vmem] * 6,
        out_specs=(anywhere,) + (vmem,) * 5,
        scratch_shapes=[pltpu.SemaphoreType.DMA],
        compiler_params=pltpu.CompilerParams(vmem_limit_bytes=VMEM_LIMIT),
    )(edge_grad, base, slot_back, indices, node_sum, w2_sum, w1_sum)
    share = width // n
    at = lax.axis_index("node") * share
    gains = lax.dynamic_slice(w2_sum, (rows_of[1], at), (2, share))
    return node_grad, edge_grad, w1_grad, w2_grad, gains[0], n1_grad, n2_grad, gains[1]


def solution(mesh):
    rows = P(("groups", "node"), None)
    flat = P(("groups", "node"))
    return jax.shard_map(
        functools.partial(local, mesh.shape["node"]),
        mesh=mesh,
        in_specs=(rows, rows, rows, rows, flat, flat, P(("groups", "node"), None, None))
        + (P(),) * 6,
        out_specs=(rows, rows, rows, rows, flat, rows, rows, flat),
        check_vma=False,
    )
```

```python
import functools
import math

import jax
import jax.numpy as jnp
from jax import lax
from jax.experimental import pallas as pl
from jax.experimental.pallas import tpu as pltpu
from jax.sharding import PartitionSpec as P

F32 = jnp.float32
BF16 = jnp.bfloat16
MESH = pl.DeviceIdType.MESH
VMEM_LIMIT = 56 * 1024 * 1024
CHUNK = 256


def mm(left, right):
    return jnp.dot(left, right, preferred_element_type=F32)


def mm_rows(left, right):
    return lax.dot_general(left, right, (((0,), (0,)), ((), ())), preferred_element_type=F32)


def mm_cols(left, right):
    return lax.dot_general(left, right, (((1,), (1,)), ((), ())), preferred_element_type=F32)


def pack(rows):
    cap, half = rows.shape[1], rows.shape[2] // 2
    return jnp.concatenate([rows[:, :, :half], rows[:, :, half:]], axis=1).astype(BF16)


def unpack(packed):
    n, cap = packed.shape[0], packed.shape[1] // 2
    wide = packed.astype(F32)
    both = jnp.concatenate([wide[:, :cap, :], wide[:, cap:, :]], axis=2)
    return both.reshape(n * cap, both.shape[2])


def swap_blocks(n, me, src, dst, send_sem, recv_sem):
    def copy_to(peer):
        return pltpu.make_async_remote_copy(
            src_ref=src.at[peer],
            dst_ref=dst.at[me],
            send_sem=send_sem.at[peer],
            recv_sem=recv_sem.at[me],
            device_id={"node": peer},
            device_id_type=MESH,
        )

    def copy_from(peer):
        return pltpu.make_async_remote_copy(
            src_ref=src.at[peer],
            dst_ref=dst.at[peer],
            send_sem=send_sem.at[peer],
            recv_sem=recv_sem.at[peer],
            device_id={"node": peer},
            device_id_type=MESH,
        )

    def start():
        @pl.loop(1, n)
        def _(k):
            copy_to(lax.rem(me + k, n)).start()

    def wait_recv():
        @pl.loop(1, n)
        def _(k):
            copy_from(lax.rem(me + k, n)).wait_recv()

    def wait_send():
        @pl.loop(1, n)
        def _(k):
            copy_from(lax.rem(me + k, n)).wait_send()

    return start, wait_recv, wait_send


def greet_all(n, me):
    barrier = pltpu.get_barrier_semaphore()

    @pl.loop(1, n)
    def _(k):
        pl.semaphore_signal(
            barrier, inc=1, device_id={"node": lax.rem(me + k, n)}, device_id_type=MESH
        )

    return barrier


def norm_back(grad, normed, inverse, gain):
    scaled = grad * gain
    first = jnp.mean(scaled, axis=-1, keepdims=True)
    second = jnp.mean(scaled * normed, axis=-1, keepdims=True)
    return inverse * (scaled - first - normed * second)


def normalize(values):
    mean = jnp.mean(values, axis=-1, keepdims=True)
    centred = values - mean
    inverse = lax.rsqrt(jnp.mean(centred * centred, axis=-1, keepdims=True) + 1e-05)
    return centred * inverse, inverse


def silu_parts(pre):
    sig = jax.nn.sigmoid(pre)
    return (pre * sig).astype(BF16), sig * (1.0 + pre * (1.0 - sig))


def bit_orders(n):
    bits = n.bit_length() - 1
    cut = 1 + (bits - 1) // 2
    low, high = list(range(1, cut)), list(range(cut, bits))
    return [0] + low + high, [0] + high + low


def place_of(d, order):
    place = 0
    for bit in order:
        place = 2 * place + ((d >> bit) & 1)
    return place


def layer_kernel(
    n,
    waves,
    node_scale,
    edge_scale,
    index_ref,
    node_ref,
    latent_ref,
    node_cot_ref,
    cot_ref,
    w1_ref,
    w2_ref,
    gain_ref,
    nw1_ref,
    nw2_ref,
    ngain_ref,
    edge_out,
    base_out,
    slot_out,
    node_sum_out,
    w2_sum_out,
    w1_sum_out,
    halo_out,
    halo_in,
    slot_send,
    slot_in,
    table,
    proj,
    pick_t,
    slope,
    hidden,
    hat,
    inv,
    rows_bf,
    agrad,
    agg_bf,
    gain_sum,
    grad_w1,
    grad_w2,
    out_send,
    out_recv,
    back_send,
    back_recv,
    wave_send,
    wave_recv,
    *buffers,
):
    me = lax.axis_index("node")
    barrier = greet_all(n, me)
    grad_n1, grad_n2 = grad_w1, grad_w2
    nodes, width = node_ref.shape
    half = width // 2
    edges = latent_ref.shape[0]
    slots = table.shape[0]
    halo = slots - nodes
    steps = edges // CHUNK
    bits = n.bit_length() - 1
    orders = bit_orders(n)
    stacks = [[buffers[2 * w + p] for p in range(2)] for w in range(3)]
    rest = buffers[6:]
    landing = [
        [[rest[(2 * w + p) * bits + level] for level in range(bits)] for p in range(2)]
        for w in range(3)
    ]
    held = [list(pair) for pair in stacks]
    bases = [[0, 0] for _ in range(3)]
    copies = {}

    def launch(w, path, level):
        bit = orders[path][level]
        mine = lax.rem(me // (1 << bit), 2)
        size = n >> (level + 1)
        peer = me + (1 - 2 * mine) * (1 << bit)
        source = held[w][path].at[pl.ds(bases[w][path] + (1 - mine) * size, size)]
        bases[w][path] = bases[w][path] + mine * size
        copy = pltpu.make_async_remote_copy(
            src_ref=source,
            dst_ref=landing[w][path][level],
            send_sem=wave_send.at[w, path, level],
            recv_sem=wave_recv.at[w, path, level],
            device_id={"node": peer},
            device_id_type=MESH,
        )
        copy.start()
        copies[w, path, level] = copy

    def advance(w, level):
        for path in range(2):
            copies[w, path, level].wait_recv()
            size = n >> (level + 1)
            base = bases[w][path]
            kept, came = held[w][path], landing[w][path][level]
            if level < bits - 1:

                @pl.loop(0, size)
                def _(k):
                    came[k] = (kept[base + k].astype(F32) + came[k].astype(F32)).astype(BF16)

                held[w][path] = came
                bases[w][path] = 0
                launch(w, path, level + 1)
            else:
                cols = slice(path * half, (path + 1) * half)
                out = (node_sum_out, w2_sum_out, w1_sum_out)[w]
                out[:, cols] = kept[base].astype(F32) + came[0].astype(F32)

    def fill(w, sources, tail):
        for path in range(2):
            cols = slice(path * half, (path + 1) * half)
            out = stacks[w][path]
            spare = out.shape[1] - sum(rows for _, _, rows in sources)
            for d in range(n):
                pieces = []
                for source, scale, rows in sources:
                    pieces.append(source[d * rows : (d + 1) * rows, cols] * scale)
                if spare:
                    pieces.append(tail[:spare, cols])
                out[place_of(d, orders[path])] = jnp.concatenate(pieces, axis=0).astype(BF16)
            launch(w, path, 0)

    node = node_ref[...]
    owner = (
        lax.broadcasted_iota(jnp.int32, (nodes, halo), 0) == index_ref[:, 2 * edges :]
    ).astype(F32).astype(BF16)
    halo_out[...] = pack(mm_rows(owner, node).reshape(n, halo // n, width))
    halo_in[me] = jnp.zeros(halo_in.shape[1:], BF16)
    slot_in[me] = jnp.zeros(slot_in.shape[1:], BF16)
    pl.semaphore_wait(barrier, n - 1)
    start, wait_in, wait_out = swap_blocks(n, me, halo_out, halo_in, out_send, out_recv)
    start()

    row_id = lax.broadcasted_iota(jnp.int32, (slots, edges), 0)
    pick_t[:slots, :] = (row_id == index_ref[:, :edges]).astype(F32).astype(BF16)
    row_id = lax.broadcasted_iota(jnp.int32, (nodes, edges), 0)
    pick_t[slots:, :] = (row_id == index_ref[:, edges : 2 * edges]).astype(F32).astype(BF16)

    @pl.loop(0, steps)
    def _(step):
        here = pl.ds(pl.multiple_of(step * CHUNK, CHUNK), CHUNK)
        slope[here, :] = mm(latent_ref[here, :], w1_ref[:width, :])

    def project(rows, value):
        high = value.astype(BF16)
        proj[rows, :width] = high
        proj[rows, width:] = (value - high.astype(F32)).astype(BF16)

    table[:nodes, :] = node
    project(slice(slots, slots + nodes), mm(node, w1_ref[2 * width :, :]))
    wait_in()
    table[nodes:, :] = unpack(halo_in[...]).astype(BF16)
    project(slice(0, slots), mm(table[...], w1_ref[width : 2 * width, :]))

    @pl.loop(0, steps)
    def _(step):
        here = pl.ds(pl.multiple_of(step * CHUNK, CHUNK), CHUNK)
        picked = mm_rows(pick_t[:, here], proj[...])
        pre = slope[here, :] + (picked[:, :width] + picked[:, width:])
        hid, slope_here = silu_parts(pre)
        hidden[here, :] = hid
        slope[here, :] = slope_here
        hat_here, inv_here = normalize(mm(hid, w2_ref[...]))
        hat[here, :] = hat_here
        inv[here, :] = inv_here
        rows_bf[here, :] = (
            latent_ref[here, :].astype(F32) + hat_here * gain_ref[...]
        ).astype(BF16)

    aggregate = mm(pick_t[slots:, :], rows_bf[...]).astype(BF16)
    node_pre = mm(node, nw1_ref[:width, :]) + mm(aggregate, nw1_ref[width:, :])
    node_hidden, node_slope = silu_parts(node_pre)
    node_hat, node_inv = normalize(mm(node_hidden, nw2_ref[...]))
    node_dy = node_cot_ref[...].astype(F32)
    node_gain_part = jnp.sum(node_dy * node_hat, axis=0, keepdims=True) * node_scale
    node_mgrad = norm_back(node_dy, node_hat, node_inv, ngain_ref[...]).astype(BF16)
    grad_n2[...] = mm_rows(node_hidden, node_mgrad)
    node_agrad = (mm_cols(node_mgrad, nw2_ref[...]) * node_slope).astype(BF16)
    grad_n1[:width, :] = mm_rows(node, node_agrad)
    grad_n1[width : 2 * width, :] = mm_rows(aggregate, node_agrad)
    blank = jnp.zeros((16, width), F32)
    n1_rows, n2_rows = 2 * width // n, width // n
    fill(0, ((grad_n1, node_scale, n1_rows), (grad_n2, node_scale, n2_rows)), blank)
    agg_bf[...] = mm_cols(node_agrad, nw1_ref[width:, :]).astype(BF16)
    base_out[...] = node_dy + mm_cols(node_agrad, nw1_ref[:width, :])
    gain_sum[...] = jnp.zeros_like(gain_sum)

    def backward(first, last):
        @pl.loop(first, last)
        def _(step):
            here = pl.ds(pl.multiple_of(step * CHUNK, CHUNK), CHUNK)
            total = cot_ref[here, :].astype(F32) + mm_rows(pick_t[slots:, here], agg_bf[...])
            hat_here = hat[here, :]
            product = total * hat_here
            gain_sum[...] += jnp.sum(product.reshape(CHUNK // 8, 8, width), axis=0)
            mgrad = norm_back(total, hat_here, inv[here, :], gain_ref[...]).astype(BF16)
            rows_bf[here, :] = mgrad
            ag = (mm_cols(mgrad, w2_ref[...]) * slope[here, :]).astype(BF16)
            agrad[here, :] = ag
            edge_out[here, :] = (total + mm_cols(ag, w1_ref[:width, :])).astype(BF16)

    third = steps // 3
    backward(0, third)
    advance(0, 0)
    backward(third, steps)

    edge_gain_part = jnp.sum(gain_sum[...], axis=0, keepdims=True) * edge_scale
    row_id = lax.broadcasted_iota(jnp.int32, (32, width), 0)
    tail = jnp.where(row_id == 0, edge_gain_part, jnp.where(row_id == 1, node_gain_part, 0.0))
    grad_w2[...] = mm_rows(hidden[...], rows_bf[...])
    fill(1, ((grad_w2, edge_scale, width // n),), tail)
    if bits > 2:
        advance(0, 1)
    sums = mm(pick_t[...], agrad[...]).astype(BF16)
    by_slot, by_target = sums[:slots, :], sums[slots:, :]
    slot_sums = mm_cols(by_slot, w1_ref[width : 2 * width, :])
    slot_send[...] = pack(slot_sums[nodes:, :].reshape(n, halo // n, width))
    back, wait_back, wait_sent = swap_blocks(n, me, slot_send, slot_in, back_send, back_recv)
    grad_w1[:width, :] = mm_rows(latent_ref[...], agrad[...])
    grad_w1[width : 2 * width, :] = mm_rows(table[...], by_slot)
    grad_w1[2 * width :, :] = mm_rows(node, by_target)
    fill(2, ((grad_w1, edge_scale, 3 * width // n),), blank)
    back()
    base_out[...] += slot_sums[:nodes, :] + mm_cols(by_target, w1_ref[2 * width :, :])

    level = [2, 0, 0]
    if bits <= 2:
        level[0] = 1
    while min(level) < bits:
        for w in (1, 0, 2):
            if level[w] < bits:
                advance(w, level[w])
                level[w] += 1
    wait_back()
    slot_out[...] = slot_in[...]
    for copy in copies.values():
        copy.wait_send()
    wait_out()
    wait_sent()


def finish_kernel(
    rows_of,
    edge_ref,
    base_ref,
    slot_ref,
    index_ref,
    node_sum,
    w2_sum,
    w1_sum,
    edge_out,
    node_out,
    w1_out,
    w2_out,
    n1_out,
    n2_out,
    sem,
):
    copy = pltpu.make_async_copy(edge_ref, edge_out, sem)
    copy.start()
    r1, r2, r3, r4 = rows_of
    nodes, halo = base_ref.shape[0], slot_ref.shape[0] * slot_ref.shape[1] // 2
    skip = index_ref.shape[1] - halo
    owner = (
        lax.broadcasted_iota(jnp.int32, (nodes, halo), 0) == index_ref[:, skip:]
    ).astype(F32).astype(BF16)
    node_out[...] = (base_ref[...] + mm(owner, unpack(slot_ref[...]).astype(BF16))).astype(BF16)
    w1_out[...] = w1_sum[:r1, :]
    w2_out[...] = w2_sum[:r2, :]
    n1_out[...] = node_sum[:r3, :]
    n2_out[...] = node_sum[r3 : r3 + r4, :]
    copy.wait()


def round_up(rows):
    return -(-rows // 16) * 16


def local(
    n,
    node_latent,
    edge_latent,
    node_cotangent,
    edge_cotangent,
    sender_slot,
    receiver,
    send_index,
    edge_w1,
    edge_w2,
    edge_gain,
    node_w1,
    node_w2,
    node_gain,
):
    nodes, width = node_latent.shape
    edges = edge_latent.shape[0]
    cap = send_index.shape[2]
    half = width // 2
    bits = n.bit_length() - 1
    node_scale = 1.0 / math.sqrt(nodes * n)
    edge_scale = 1.0 / math.sqrt(edges * n)
    rows_of = tuple(w.shape[0] // n for w in (edge_w1, edge_w2, node_w1, node_w2))
    waves = (
        round_up(rows_of[2] + rows_of[3]),
        round_up(rows_of[1] + 2),
        round_up(rows_of[0]),
    )
    slots = nodes + n * cap
    vmem = pl.BlockSpec(memory_space=pltpu.VMEM)
    anywhere = pl.BlockSpec(memory_space=pl.ANY)
    packed = jax.ShapeDtypeStruct((n, 2 * cap, half), BF16)
    indices = jnp.concatenate([sender_slot, receiver, send_index.reshape(n * cap)]).reshape(1, -1)
    stacks = [pltpu.VMEM((n, block, half), BF16) for block in waves for _ in range(2)]
    landing = [
        pltpu.VMEM((n >> (level + 1), block, half), BF16)
        for block in waves
        for _ in range(2)
        for level in range(bits)
    ]

    edge_grad, base, slot_back, node_sum, w2_sum, w1_sum = pl.pallas_call(
        functools.partial(layer_kernel, n, waves, node_scale, edge_scale),
        out_shape=(
            jax.ShapeDtypeStruct((edges, width), BF16),
            jax.ShapeDtypeStruct((nodes, width), F32),
            packed,
        )
        + tuple(jax.ShapeDtypeStruct((block, width), F32) for block in waves),
        in_specs=[vmem] * 11,
        out_specs=(vmem,) * 6,
        scratch_shapes=[pltpu.VMEM(packed.shape, BF16)] * 4
        + [
            pltpu.VMEM((slots, width), BF16),
            pltpu.VMEM((slots + nodes, 2 * width), BF16),
            pltpu.VMEM((slots + nodes, edges), BF16),
            pltpu.VMEM((edges, width), F32),
            pltpu.VMEM((edges, width), BF16),
            pltpu.VMEM((edges, width), F32),
            pltpu.VMEM((edges, 1), F32),
            pltpu.VMEM((edges, width), BF16),
            pltpu.VMEM((edges, width), BF16),
            pltpu.VMEM((nodes, width), BF16),
            pltpu.VMEM((8, width), F32),
            pltpu.VMEM((3 * width, width), F32),
            pltpu.VMEM((width, width), F32),
        ]
        + [pltpu.SemaphoreType.DMA((n,))] * 4
        + [pltpu.SemaphoreType.DMA((3, 2, bits))] * 2
        + stacks
        + landing,
        compiler_params=pltpu.CompilerParams(
            collective_id=0, has_side_effects=True, vmem_limit_bytes=VMEM_LIMIT
        ),
    )(
        indices,
        node_latent,
        edge_latent,
        node_cotangent,
        edge_cotangent,
        edge_w1,
        edge_w2,
        edge_gain.reshape(1, width),
        node_w1,
        node_w2,
        node_gain.reshape(1, width),
    )

    edge_grad, node_grad, w1_grad, w2_grad, n1_grad, n2_grad = pl.pallas_call(
        functools.partial(finish_kernel, rows_of),
        out_shape=(
            jax.ShapeDtypeStruct((edges, width), BF16),
            jax.ShapeDtypeStruct((nodes, width), BF16),
        )
        + tuple(jax.ShapeDtypeStruct((rows, width), F32) for rows in rows_of),
        in_specs=[vmem] * 7,
        out_specs=(anywhere,) + (vmem,) * 5,
        scratch_shapes=[pltpu.SemaphoreType.DMA],
        compiler_params=pltpu.CompilerParams(vmem_limit_bytes=VMEM_LIMIT),
    )(edge_grad, base, slot_back, indices, node_sum, w2_sum, w1_sum)
    share = width // n
    at = lax.axis_index("node") * share
    gains = lax.dynamic_slice(w2_sum, (rows_of[1], at), (2, share))
    return node_grad, edge_grad, w1_grad, w2_grad, gains[0], n1_grad, n2_grad, gains[1]


def solution(mesh):
    rows = P(("groups", "node"), None)
    flat = P(("groups", "node"))
    return jax.shard_map(
        functools.partial(local, mesh.shape["node"]),
        mesh=mesh,
        in_specs=(rows, rows, rows, rows, flat, flat, P(("groups", "node"), None, None))
        + (P(),) * 6,
        out_specs=(rows, rows, rows, rows, flat, rows, rows, flat),
        check_vma=False,
    )
```
